32 devices in a mesh: group: 2 (over x), expert: 16 (over z, y, core), dp: 1.
Axes of the slice: x: 2, y: 2, z: 4, core: 2. Of those that a mesh axis runs over, the one named last changes fastest.
Arguments:
- gate_update: bfloat16 [16, 4096, 768], P(None, ('expert', 'dp')), may hold values from -0.09375 to 0.09375
- up_update: bfloat16 [16, 4096, 768], P(None, ('expert', 'dp')), may hold values from -0.09375 to 0.09375
- down_weight: bfloat16 [16, 768, 4096], P('expert', 'dp'), may hold values from -0.21875 to 0.21875
- out_proj: bfloat16 [8192, 4096], P('expert'), may hold values from -0.0625 to 0.0625
- norm_gain: float32 [4096], replicated, may hold values from 0.1 to 1.9
- residual: bfloat16 [2, 2, 64, 4096], P(None, ('group', 'dp'), 'expert'), parts along dimension 1, may hold values from -4 to 4
- queries: bfloat16 [2, 2, 64, 8192], P(None, ('group', 'dp'), 'expert'), parts along dimension 1, may hold values from -150 to 150
- token_keys: bfloat16 [2, 2, 64, 512], P(None, ('group', 'dp'), 'expert'), parts along dimension 1, may hold values from -6 to 6
- token_values: bfloat16 [2, 2, 64, 512], P(None, ('group', 'dp'), 'expert'), parts along dimension 1, may hold values from -6 to 6
- cached_key_rows: bfloat16 [2, 64, 192, 512], P(('group', 'dp'), 'expert'), parts along dimension 0, may hold values from -6 to 6
- cached_value_rows: bfloat16 [2, 64, 192, 512], P(('group', 'dp'), 'expert'), parts along dimension 0, may hold values from -6 to 6
- lengths: int32 [2, 64], P(('group', 'dp'), 'expert'), parts along dimension 0, may hold values from 2 to 192, as said below
- expert_ids: int32 [2, 2, 64, 8], P(None, ('group', 'dp'), 'expert'), parts along dimension 1, may hold values from 0 to 15, all different within a row; in each aligned block of 4 rows (0 to 3, 4 to 7, ..., all dimensions but the last counted through in order) at most 3 rows name the same one
- gate_probs: float32 [2, 2, 64, 8], P(None, ('group', 'dp'), 'expert'), parts along dimension 1, may hold values from 0.02 to 0.5
Outputs:
- stream: bfloat16 [2, 2, 64, 4096], P(None, ('group', 'dp'), 'expert'), parts along dimension 1
- mixed: bfloat16 [2, 2, 64, 4096], P(None, ('group', 'dp'), 'expert'), parts along dimension 1
The draws below stay inside these ranges and needn't reach their ends.
There are 2 independent parts, one for each index of `group`. The reference program is written for one: setup_inputs(seed, part) draws one part's arguments, and reference() takes and returns one part's arrays. A program takes and returns all parts, laid end to end along the dimension named above; an argument that names none is the same for every part. Nothing has to cross between parts.
Inputs may be any that keep to these rules, and one draw needn't show every extreme that they name: `lengths`: cache slots at and beyond a row's length are not used. `expert_ids`: each row names 8 different experts; within the rows of one device in one step no expert is named by more than 3 rows.
All inputs are finite; a program needn't handle non-finite values.
Results may differ from the reference program's by a relative error of at most 0.04.
Values may be sent and summed in bfloat16 or wider, within the bound.
A program may use at most 128 MiB of HBM per device.

```python
import math
import jax
import jax.numpy as jnp
import numpy as np
from jax import lax

D = 4096
QUERY_HEADS = 64
KEY_VALUE_HEADS = 4
HEAD_SIZE = 128
TOPK = 8
FFW = 768
DECODE_STEPS = 2
ROWS_DEV = 4
CACHE_SLOTS = 192
EXPERTS = 16
BATCH_ROWS = 64
ROW_BATCHES = 1
CAP = 3
N_EXPERT = 16


def shared_keys(key):
    base_offset = jax.random.normal(key, (ROW_BATCHES, BATCH_ROWS, CACHE_SLOTS, KEY_VALUE_HEADS * HEAD_SIZE), jnp.float32)
    return jnp.clip(base_offset, -6.0, 6.0)


def draw_cached_key_rows(key, part):
    base_offset = shared_keys(key)
    return base_offset.astype(jnp.bfloat16)


def draw_queries(key, part):
    key = jax.random.fold_in(key, 7)
    drawn = jnp.clip(jax.random.normal(key, (DECODE_STEPS, ROW_BATCHES, BATCH_ROWS, QUERY_HEADS * HEAD_SIZE), jnp.float32), -6.0, 6.0)
    return drawn.astype(jnp.bfloat16)


def draw_lengths(key, part):
    key = jax.random.fold_in(key, 9)
    first_key, second_key = jax.random.split(key)
    device_top = jax.random.randint(first_key, (ROW_BATCHES, BATCH_ROWS // ROWS_DEV, 1), max(2, CACHE_SLOTS // 4), CACHE_SLOTS + 1)
    raw = jax.random.randint(second_key, (ROW_BATCHES, BATCH_ROWS // ROWS_DEV, ROWS_DEV), 0, 1 << 20)
    picked = 2 + raw % (device_top - 1)
    picked = picked.reshape(ROW_BATCHES, BATCH_ROWS).astype(jnp.int32)
    picked = picked.at[0, 0].set(CACHE_SLOTS)
    return picked.at[0, 1].set(2)


def steps_of(key, extent, pieces, least, largest):
    loudness = 1.0
    for position, parts in pieces:
        draws = jax.random.uniform(jax.random.fold_in(jax.random.fold_in(key, 6), position), (parts,), jnp.float32, least / len(pieces), largest / len(pieces))
        loudness = loudness * jnp.repeat(jnp.exp(draws), extent[position] // parts).reshape((-1,) + (1,) * (len(extent) - 1 - position))
    return loudness


def deal_out(stream_key, own, number, rows, amount, top, bound, lean):
    order = jax.random.permutation(stream_key, amount)
    crowded, common = shares(amount, rows * top, bound, lean, True), shares(amount, rows * top, bound, lean, False)
    places = jnp.arange(amount)

    def named(sizes, offset_by):
        used = int((sizes > 0).sum())
        fixed = max(1, used // 4)
        passed = fixed + (places - fixed + offset_by * (used - fixed)) % max(1, amount - fixed)
        return jnp.zeros((amount,), jnp.int32).at[order[jnp.where(places < fixed, places, passed)]].set(jnp.asarray(sizes, jnp.int32))

    sizes = jnp.where(number % 4 == 0, named(crowded, number // 4), named(common, number - number // 4 - 1))
    mixed = jax.random.permutation(jax.random.fold_in(own, 3), amount)
    giver, taker = mixed[0:amount // 2 * 2:2], mixed[1:amount // 2 * 2:2]
    slack = jnp.minimum(sizes[giver] - 1, bound - sizes[taker]) // 2
    slack = jnp.where((giver == order[0]) | (taker == order[0]) | (sizes[taker] == 0), 0, jnp.maximum(slack, 0))
    passed = jax.random.randint(jax.random.fold_in(own, 4), (amount // 2,), 0, 1 << 20) % (slack + 1)
    sizes = sizes.at[giver].add(-passed).at[taker].add(passed)
    labels = jnp.searchsorted(jnp.cumsum(sizes), jnp.arange(rows * top), side="right").astype(jnp.int32)
    table = labels.reshape(top, rows).T
    table = table[jax.random.permutation(jax.random.fold_in(own, 1), rows)]
    offset_by = jax.random.randint(jax.random.fold_in(own, 2), (rows, 1), 0, top)
    return jnp.take_along_axis(table, (jnp.arange(top)[None, :] + offset_by) % top, axis=1)


def shares(amount, total, bound, lean, full):
    weights = [(1 << 20) // math.isqrt(standing ** lean) + 1 for standing in range(1, amount + 1)]
    largest = bound if full else min(bound, max(-(-total // amount), total * weights[0] // sum(weights)))
    least = 1 if total - largest >= amount - 1 else 0
    given, spare = [largest] + [least] * (amount - 1), total - largest - least * (amount - 1)
    while spare > 0:
        candidates = [i for i in range(1, amount) if given[i] < largest] or [i for i in range(1, amount) if given[i] < bound]
        whole, remaining = sum([weights[i] for i in candidates]), spare
        for i in candidates:
            addition = min(bound - given[i], max(1, remaining * weights[i] // whole), spare)
            given[i] = given[i] + addition
            spare = spare - addition
    return np.array(given)


def gaussian(rng, extent, scale, most, shards=(), held_as=jnp.bfloat16):
    result = jax.random.normal(rng, extent, jnp.float32) * scale
    if len(shards) > 0:
        result = steps_of(rng, extent, shards, -0.22, 0.18) * result
    return jnp.clip(result, min=-most, max=most).astype(held_as)


def setup_inputs(seed: int = 0, part: int = 0) -> dict:
    key_of = jax.random.split(jax.random.key(seed), 15)
    own_keys = jax.random.split(jax.random.fold_in(key_of[14], part), 15)
    gate_update = gaussian(key_of[0], (EXPERTS, D, FFW), D ** -0.5, 0.09375, ((1, 16),))
    up_update = gaussian(key_of[1], (EXPERTS, D, FFW), D ** -0.5, 0.09375, ((1, 16),))
    down_weight = gaussian(key_of[2], (EXPERTS, FFW, D), FFW ** -0.5, 0.21875, ((0, 16),))
    out_proj = gaussian(key_of[3], (QUERY_HEADS * HEAD_SIZE, D), (QUERY_HEADS * HEAD_SIZE) ** -0.5, 0.0625, ((0, 16),))
    norm_gain = jnp.clip(1.0 + 0.18 * jax.random.normal(key_of[4], (D,), jnp.float32), 0.1, 1.9)
    residual = gaussian(own_keys[5], (DECODE_STEPS, ROW_BATCHES, BATCH_ROWS, D), 0.25, 4.0, ((2, 16),))
    queries = draw_queries(jax.random.fold_in(jax.random.fold_in(key_of[14], part), 71), part)
    token_keys = gaussian(own_keys[7], (DECODE_STEPS, ROW_BATCHES, BATCH_ROWS, KEY_VALUE_HEADS * HEAD_SIZE), 1.0, 6.0, ((2, 16),))
    token_values = gaussian(own_keys[8], (DECODE_STEPS, ROW_BATCHES, BATCH_ROWS, KEY_VALUE_HEADS * HEAD_SIZE), 1.0, 6.0, ((2, 16),))
    cached_key_rows = draw_cached_key_rows(jax.random.fold_in(jax.random.fold_in(key_of[14], part), 71), part)
    cached_value_rows = gaussian(own_keys[10], (ROW_BATCHES, BATCH_ROWS, CACHE_SLOTS, KEY_VALUE_HEADS * HEAD_SIZE), 1.0, 6.0, ((1, 16),))
    lengths = draw_lengths(jax.random.fold_in(jax.random.fold_in(key_of[14], part), 71), part)
    expert_ids_keys = jax.random.split(jax.random.fold_in(own_keys[12], 1), DECODE_STEPS * ROW_BATCHES * BATCH_ROWS // ROWS_DEV)
    expert_ids_turns = jax.random.permutation(jax.random.fold_in(own_keys[12], 3), DECODE_STEPS * ROW_BATCHES * BATCH_ROWS // ROWS_DEV)
    expert_ids = jax.vmap(lambda own, number: deal_out(jax.random.fold_in(own_keys[12], 2), own, number, ROWS_DEV, EXPERTS, TOPK, CAP, 2))(expert_ids_keys, expert_ids_turns).reshape((DECODE_STEPS, ROW_BATCHES, BATCH_ROWS, TOPK))
    gate_probs = jnp.clip(jnp.exp(math.log(0.5) - 3.218876 * jax.random.uniform(own_keys[13], (DECODE_STEPS, ROW_BATCHES, BATCH_ROWS, TOPK), jnp.float32) ** steps_of(own_keys[13], (DECODE_STEPS, ROW_BATCHES, BATCH_ROWS, TOPK), ((2, 16),), -0.2, 0.2)), 0.02, 0.5)
    return dict(gate_update=gate_update, up_update=up_update, down_weight=down_weight, out_proj=out_proj, norm_gain=norm_gain, residual=residual, queries=queries, token_keys=token_keys, token_values=token_values, cached_key_rows=cached_key_rows, cached_value_rows=cached_value_rows, lengths=lengths, expert_ids=expert_ids, gate_probs=gate_probs)


def expert_branch(normed, chosen_ids, chosen_probs, gate_update, up_update, down_weight, count_of_rows, limit):
    flat_ids = chosen_ids.reshape(-1).astype(jnp.int32)
    pick_rows = (jnp.arange(count_of_rows * TOPK, dtype=jnp.int32) // TOPK).astype(jnp.int32)
    onehot = (flat_ids[:, None] == jnp.arange(EXPERTS, dtype=jnp.int32)[None, :]).astype(jnp.int32)
    before = jnp.cumsum(onehot, axis=0) - onehot
    slot_rank = lax.optimization_barrier(jnp.sum(before * onehot, axis=1)).astype(jnp.int32)
    table = jnp.full((EXPERTS, limit), count_of_rows, jnp.int32).at[flat_ids, slot_rank].set(pick_rows)
    padded = jnp.concatenate([normed, jnp.zeros((1, D), jnp.bfloat16)], axis=0)

    def run_expert(expert_index):
        chosen = padded[table[expert_index]]
        gate_part = jnp.dot(chosen, gate_update[expert_index], preferred_element_type=jnp.float32)
        up_part = jnp.dot(chosen, up_update[expert_index], preferred_element_type=jnp.float32)
        hidden = (jax.nn.silu(gate_part) * up_part).astype(jnp.bfloat16)
        return jnp.dot(hidden, down_weight[expert_index], preferred_element_type=jnp.float32).astype(jnp.bfloat16)
    outputs = lax.map(run_expert, jnp.arange(EXPERTS, dtype=jnp.int32))
    picked = outputs[flat_ids, slot_rank].astype(jnp.float32).reshape(count_of_rows, TOPK, D)
    weighted = picked * chosen_probs.reshape(count_of_rows, TOPK, 1).astype(jnp.float32)
    return lax.optimization_barrier(jnp.sum(weighted, axis=1)).astype(jnp.bfloat16)

def reference(gate_update, up_update, down_weight, out_proj, norm_gain, residual, queries, token_keys, token_values, cached_key_rows, cached_value_rows, lengths, expert_ids, gate_probs):
    count_of_rows = ROW_BATCHES * BATCH_ROWS
    head_groups = QUERY_HEADS // KEY_VALUE_HEADS
    score_scale = 1.0 / math.sqrt(HEAD_SIZE)
    limit = count_of_rows // ROWS_DEV * CAP
    key_cache_table = cached_key_rows.reshape(count_of_rows, CACHE_SLOTS, KEY_VALUE_HEADS, HEAD_SIZE).astype(jnp.float32)
    value_cache_table = cached_value_rows.reshape(count_of_rows, CACHE_SLOTS, KEY_VALUE_HEADS, HEAD_SIZE).astype(jnp.float32)
    cache_valid = jnp.arange(CACHE_SLOTS, dtype=jnp.int32)[None, :] < lengths.reshape(count_of_rows)[:, None]
    proj_blocks = out_proj.reshape(N_EXPERT, QUERY_HEADS * HEAD_SIZE // N_EXPERT, D).astype(jnp.float32)
    streams = []
    mixes = []
    for decode_step_index in range(DECODE_STEPS):
        query_matrix = queries[decode_step_index].reshape(count_of_rows, KEY_VALUE_HEADS, head_groups, HEAD_SIZE).astype(jnp.float32)
        incoming_keys = token_keys[:decode_step_index + 1].reshape(decode_step_index + 1, count_of_rows, KEY_VALUE_HEADS, HEAD_SIZE).astype(jnp.float32)
        incoming_values = token_values[:decode_step_index + 1].reshape(decode_step_index + 1, count_of_rows, KEY_VALUE_HEADS, HEAD_SIZE).astype(jnp.float32)
        all_keys = jnp.concatenate([key_cache_table, jnp.transpose(incoming_keys, (1, 0, 2, 3))], axis=1)
        all_values = jnp.concatenate([value_cache_table, jnp.transpose(incoming_values, (1, 0, 2, 3))], axis=1)
        valid = jnp.concatenate([cache_valid, jnp.ones((count_of_rows, decode_step_index + 1), bool)], axis=1)
        scores = jnp.einsum('rhgd,rlhd->rhgl', query_matrix, all_keys) * score_scale
        scores = jnp.where(valid[:, None, None, :], scores, -1e+30)
        weights = jax.nn.softmax(scores, axis=-1).astype(jnp.bfloat16)
        attended = jnp.einsum('rhgl,rlhd->rhgd', weights.astype(jnp.float32), all_values).astype(jnp.bfloat16)
        blocks = attended.reshape(count_of_rows, N_EXPERT, QUERY_HEADS * HEAD_SIZE // N_EXPERT).astype(jnp.float32)
        partial_sums = jnp.einsum('rgc,gcd->rgd', blocks, proj_blocks).astype(jnp.bfloat16)
        combined = lax.optimization_barrier(jnp.sum(partial_sums.astype(jnp.float32), axis=1))
        stream_now = residual[decode_step_index].reshape(count_of_rows, D).astype(jnp.float32) + combined
        stream_now = stream_now.astype(jnp.bfloat16)
        wide = stream_now.astype(jnp.float32)
        mean_square = lax.optimization_barrier(jnp.mean(wide * wide, axis=-1, keepdims=True))
        normed = (wide * lax.rsqrt(mean_square + 1e-06) * norm_gain.astype(jnp.float32)[None, :]).astype(jnp.bfloat16)
        mixed_now = expert_branch(normed, expert_ids[decode_step_index], gate_probs[decode_step_index], gate_update, up_update, down_weight, count_of_rows, limit)
        streams.append(stream_now)
        mixes.append(mixed_now)
    stream = jnp.stack(streams).reshape(DECODE_STEPS, ROW_BATCHES, BATCH_ROWS, D)
    mixed = jnp.stack(mixes).reshape(DECODE_STEPS, ROW_BATCHES, BATCH_ROWS, D)
    return (stream, mixed)
```

```python
import math

import jax
import jax.numpy as jnp
from jax import lax
from jax.sharding import PartitionSpec as P

QUERY_HEADS = 64
KEY_VALUE_HEADS = 4
HEAD_SIZE = 128
F32 = jnp.float32
BF16 = jnp.bfloat16


def scatter_sum(x, axis_name, order):
    count = x.shape[0]
    bits = count.bit_length() - 1
    if bits == 0:
        return x[0]
    me = lax.axis_index(axis_name)
    x = x.reshape((2,) * bits + x.shape[1:])
    left = list(range(bits - 1, -1, -1))
    for bit in order(bits):
        at = left.index(bit)
        left.pop(at)
        mine = (me >> bit) & 1
        keep = lax.dynamic_index_in_dim(x, mine, at, keepdims=False)
        send = lax.dynamic_index_in_dim(x, 1 - mine, at, keepdims=False)
        got = lax.ppermute(send, axis_name, [(i, i ^ (1 << bit)) for i in range(count)])
        x = (keep.astype(F32) + got.astype(F32)).astype(BF16)
    return x


def near_first(bits):
    return list(range(bits))


def far_first(bits):
    return [0] + list(range(2, bits)) + [1] if bits > 2 else list(range(bits))


def scatter_both(x, order):
    if x.shape[1] > 1:
        x = scatter_sum(jnp.moveaxis(x, 1, 0), "dp", near_first)
    else:
        x = x[:, 0]
    return scatter_sum(x, "expert", order)


def attend(queries, token_keys, token_values, key_rows, value_rows, lengths):
    steps, rows = queries.shape[0], queries.shape[2]
    slots = key_rows.shape[2]
    per = QUERY_HEADS // KEY_VALUE_HEADS
    q = queries[:, 0].reshape(steps, rows, KEY_VALUE_HEADS, per, HEAD_SIZE)
    kc = key_rows[0].reshape(rows, slots, KEY_VALUE_HEADS, HEAD_SIZE)
    vc = value_rows[0].reshape(rows, slots, KEY_VALUE_HEADS, HEAD_SIZE)
    kt = token_keys[:, 0].reshape(steps, rows, KEY_VALUE_HEADS, HEAD_SIZE)
    vt = token_values[:, 0].reshape(steps, rows, KEY_VALUE_HEADS, HEAD_SIZE)
    scale = 1.0 / math.sqrt(HEAD_SIZE)
    sc = jnp.einsum("srhgd,rlhd->rhsgl", q, kc, preferred_element_type=F32) * scale
    sf = jnp.einsum("srhgd,lrhd->rhsgl", q, kt, preferred_element_type=F32) * scale
    valid = jnp.arange(slots, dtype=jnp.int32)[None, :] < lengths[0][:, None]
    causal = jnp.arange(steps)[None, :] <= jnp.arange(steps)[:, None]
    sc = jnp.where(valid[:, None, None, None, :], sc, -1e30)
    sf = jnp.where(causal[None, None, :, None, :], sf, -1e30)
    peak = jnp.maximum(jnp.max(sc, -1, keepdims=True), jnp.max(sf, -1, keepdims=True))
    ec, ef = jnp.exp(sc - peak), jnp.exp(sf - peak)
    total = jnp.sum(ec, -1, keepdims=True) + jnp.sum(ef, -1, keepdims=True)
    wc, wf = (ec / total).astype(BF16), (ef / total).astype(BF16)
    out = jnp.einsum("rhsgl,rlhd->srhgd", wc, vc, preferred_element_type=F32)
    out = out + jnp.einsum("rhsgl,lrhd->srhgd", wf, vt, preferred_element_type=F32)
    return out.astype(BF16).reshape(steps * rows, QUERY_HEADS * HEAD_SIZE)


def shards(
    gate_update,
    up_update,
    down_weight,
    out_proj,
    norm_gain,
    residual,
    queries,
    token_keys,
    token_values,
    cached_key_rows,
    cached_value_rows,
    lengths,
    expert_ids,
    gate_probs,
):
    experts, depth, units = gate_update.shape
    ring = lax.axis_size("expert")
    pair = lax.axis_size("dp")
    steps, _, rows, width = residual.shape
    top = expert_ids.shape[3]
    own = steps * rows
    me, half = lax.axis_index("expert"), lax.axis_index("dp")

    ids = expert_ids.reshape(own, top)
    probs = gate_probs.reshape(own, top)
    match = ids[:, :, None] == jnp.arange(experts, dtype=jnp.int32)[None, None, :]
    coefs = jnp.sum(jnp.where(match, probs[:, :, None], 0.0), axis=1)
    coefs = lax.all_gather(coefs.T, ("expert", "dp"), axis=0)
    coefs = lax.dynamic_index_in_dim(coefs, me, 1, keepdims=False)
    coefs = coefs.reshape(ring, pair, own).swapaxes(0, 1).reshape(-1)

    attended = attend(queries, token_keys, token_values, cached_key_rows, cached_value_rows, lengths)
    spread = lax.all_to_all(attended, "expert", split_axis=1, concat_axis=0, tiled=True)
    partial = jnp.dot(spread, out_proj, preferred_element_type=F32)
    place = (jnp.arange(ring) == me).astype(F32)
    partial = partial.reshape(ring, own, width) + place[:, None, None] * residual.reshape(1, own, width).astype(F32)
    partial = partial.astype(BF16).reshape(ring * own, ring, width // ring).swapaxes(0, 1)
    columns = scatter_sum(partial, "expert", near_first)
    back = lax.all_to_all(columns, "expert", split_axis=0, concat_axis=1, tiled=True)
    stream = back.reshape(residual.shape)
    if pair > 1:
        columns = lax.all_to_all(columns, "dp", split_axis=1, concat_axis=0, tiled=True)

    wide = columns.astype(F32)
    square = lax.psum(jnp.sum(wide * wide, axis=1), ("expert", "dp"))
    scale = lax.rsqrt(square / width + 1e-6)[:, None]
    gain = lax.dynamic_slice_in_dim(norm_gain, (me * pair + half) * depth, depth)
    scaled = (wide * gain[None, :]).astype(BF16)
    all_rows = scaled.shape[0]

    def project(chosen, weight, order):
        sums = jnp.einsum("rd,edf->erf", chosen, weight, preferred_element_type=F32).astype(BF16)
        sums = sums.reshape(experts, chosen.shape[0], pair, units // pair).swapaxes(1, 2)
        return scatter_both(sums, order)

    def both(chosen):
        return project(chosen, gate_update, near_first), project(chosen, up_update, far_first)

    if all_rows <= 128:
        gate, up = both(scaled)
    else:
        gate, up = lax.map(both, scaled.reshape(-1, 128, depth))
    gate = gate.reshape(all_rows, -1).astype(F32) * scale
    up = up.reshape(all_rows, -1).astype(F32) * scale
    hidden = (jax.nn.silu(gate) * up * coefs[:, None]).astype(BF16)
    out = jnp.dot(hidden, down_weight[0], preferred_element_type=F32).astype(BF16)
    out = out.reshape(pair, ring, own, width).swapaxes(0, 1)
    mixed = scatter_both(out, near_first).reshape(residual.shape)
    return (stream, mixed)


def solution(mesh):
    in_specs = (
        P(None, ("expert", "dp"), None),
        P(None, ("expert", "dp"), None),
        P("expert", "dp", None),
        P("expert", None),
        P(),
        P(None, ("group", "dp"), "expert", None),
        P(None, ("group", "dp"), "expert", None),
        P(None, ("group", "dp"), "expert", None),
        P(None, ("group", "dp"), "expert", None),
        P(("group", "dp"), "expert", None, None),
        P(("group", "dp"), "expert", None, None),
        P(("group", "dp"), "expert"),
        P(None, ("group", "dp"), "expert", None),
        P(None, ("group", "dp"), "expert", None),
    )
    out_specs = (P(None, ("group", "dp"), "expert", None), P(None, ("group", "dp"), "expert", None))
    return jax.shard_map(shards, mesh=mesh, in_specs=in_specs, out_specs=out_specs, check_vma=False)
```

```python
import math

import jax
import jax.numpy as jnp
from jax import lax
from jax.sharding import PartitionSpec as P

QUERY_HEADS = 64
KEY_VALUE_HEADS = 4
HEAD_SIZE = 128
F32 = jnp.float32
BF16 = jnp.bfloat16


def scatter_sum(x, axis_name, order):
    count = x.shape[0]
    bits = count.bit_length() - 1
    if bits == 0:
        return x[0]
    me = lax.axis_index(axis_name)
    x = x.reshape((2,) * bits + x.shape[1:])
    left = list(range(bits - 1, -1, -1))
    for bit in order(bits):
        at = left.index(bit)
        left.pop(at)
        mine = (me >> bit) & 1
        keep = lax.dynamic_index_in_dim(x, mine, at, keepdims=False)
        send = lax.dynamic_index_in_dim(x, 1 - mine, at, keepdims=False)
        got = lax.ppermute(send, axis_name, [(i, i ^ (1 << bit)) for i in range(count)])
        x = (keep.astype(F32) + got.astype(F32)).astype(BF16)
    return x


def add_up(x):
    if lax.axis_size("dp") > 1:
        x = lax.psum(x, "dp")
    count = lax.axis_size("expert")
    for bit in range(count.bit_length() - 1):
        x = x + lax.ppermute(x, "expert", [(i, i ^ (1 << bit)) for i in range(count)])
    return x


def near_first(bits):
    return list(range(bits))


def far_first(bits):
    return [0] + list(range(2, bits)) + [1] if bits > 2 else list(range(bits))


def scatter_both(x, order):
    if x.shape[1] > 1:
        x = scatter_sum(jnp.moveaxis(x, 1, 0), "dp", near_first)
    else:
        x = x[:, 0]
    return scatter_sum(x, "expert", order)


def attend(queries, token_keys, token_values, key_rows, value_rows, lengths):
    steps, rows = queries.shape[0], queries.shape[2]
    slots = key_rows.shape[2]
    per = QUERY_HEADS // KEY_VALUE_HEADS
    q = queries[:, 0].reshape(steps, rows, KEY_VALUE_HEADS, per, HEAD_SIZE)
    kc = key_rows[0].reshape(rows, slots, KEY_VALUE_HEADS, HEAD_SIZE)
    vc = value_rows[0].reshape(rows, slots, KEY_VALUE_HEADS, HEAD_SIZE)
    kt = token_keys[:, 0].reshape(steps, rows, KEY_VALUE_HEADS, HEAD_SIZE)
    vt = token_values[:, 0].reshape(steps, rows, KEY_VALUE_HEADS, HEAD_SIZE)
    scale = 1.0 / math.sqrt(HEAD_SIZE)
    sc = jnp.einsum("srhgd,rlhd->rhsgl", q, kc, preferred_element_type=F32) * scale
    sf = jnp.einsum("srhgd,lrhd->rhsgl", q, kt, preferred_element_type=F32) * scale
    valid = jnp.arange(slots, dtype=jnp.int32)[None, :] < lengths[0][:, None]
    causal = jnp.arange(steps)[None, :] <= jnp.arange(steps)[:, None]
    sc = jnp.where(valid[:, None, None, None, :], sc, -1e30)
    sf = jnp.where(causal[None, None, :, None, :], sf, -1e30)
    peak = jnp.maximum(jnp.max(sc, -1, keepdims=True), jnp.max(sf, -1, keepdims=True))
    ec, ef = jnp.exp(sc - peak), jnp.exp(sf - peak)
    total = jnp.sum(ec, -1, keepdims=True) + jnp.sum(ef, -1, keepdims=True)
    wc, wf = (ec / total).astype(BF16), (ef / total).astype(BF16)
    out = jnp.einsum("rhsgl,rlhd->srhgd", wc, vc, preferred_element_type=F32)
    out = out + jnp.einsum("rhsgl,lrhd->srhgd", wf, vt, preferred_element_type=F32)
    return out.astype(BF16).reshape(steps * rows, QUERY_HEADS * HEAD_SIZE)


def shards(
    gate_update,
    up_update,
    down_weight,
    out_proj,
    norm_gain,
    residual,
    queries,
    token_keys,
    token_values,
    cached_key_rows,
    cached_value_rows,
    lengths,
    expert_ids,
    gate_probs,
):
    experts, depth, units = gate_update.shape
    ring = lax.axis_size("expert")
    pair = lax.axis_size("dp")
    steps, _, rows, width = residual.shape
    top = expert_ids.shape[3]
    own = steps * rows
    me, half = lax.axis_index("expert"), lax.axis_index("dp")

    ids = expert_ids.reshape(own, top)
    probs = gate_probs.reshape(own, top)
    match = ids[:, :, None] == jnp.arange(experts, dtype=jnp.int32)[None, None, :]
    coefs = jnp.sum(jnp.where(match, probs[:, :, None], 0.0), axis=1)
    coarse = coefs.astype(BF16)
    fine = (coefs - coarse.astype(F32)).astype(BF16)
    lanes = -(-2 * experts // 128) * 128
    extra = jnp.pad(jnp.concatenate([coarse, fine], axis=1), ((0, 0), (0, lanes - 2 * experts)))

    attended = attend(queries, token_keys, token_values, cached_key_rows, cached_value_rows, lengths)
    packed = jnp.concatenate(
        [attended.reshape(own, ring, -1), jnp.broadcast_to(extra[:, None], (own, ring, lanes))], axis=2
    )
    spread = lax.all_to_all(
        packed.reshape(own, -1), "expert", split_axis=1, concat_axis=0, tiled=True
    )
    heads = out_proj.shape[0]
    coefs = spread[:, heads:].astype(F32)
    coefs = coefs[:, :experts] + coefs[:, experts : 2 * experts]
    coefs = lax.dynamic_index_in_dim(coefs, me, 1, keepdims=False)
    if pair > 1:
        coefs = lax.all_gather(coefs, "dp", axis=0, tiled=True)
    spread = spread[:, :heads]
    partial = jnp.dot(spread, out_proj, preferred_element_type=F32)
    place = (jnp.arange(ring) == me).astype(F32)
    partial = partial.reshape(ring, own, width) + place[:, None, None] * residual.reshape(1, own, width).astype(F32)
    partial = partial.astype(BF16).reshape(ring * own, ring, width // ring).swapaxes(0, 1)
    middle = partial.shape[1] // 2
    columns = jnp.concatenate(
        [
            scatter_sum(partial[:, :middle], "expert", near_first),
            scatter_sum(partial[:, middle:], "expert", far_first),
        ],
        axis=0,
    )
    back = lax.all_to_all(columns, "expert", split_axis=0, concat_axis=1, tiled=True)
    if pair > 1:
        columns = lax.all_to_all(columns, "dp", split_axis=1, concat_axis=0, tiled=True)

    wide = columns.astype(F32)
    square = add_up(jnp.sum(wide * wide, axis=1))
    scale = lax.rsqrt(square / width + 1e-6)[:, None]
    gain = lax.dynamic_slice_in_dim(norm_gain, (me * pair + half) * depth, depth)
    scaled = (wide * gain[None, :]).astype(BF16)
    all_rows = scaled.shape[0]

    def project(chosen, weight, order):
        sums = jnp.einsum("rd,edf->erf", chosen, weight, preferred_element_type=F32).astype(BF16)
        sums = sums.reshape(experts, chosen.shape[0], pair, units // pair).swapaxes(1, 2)
        return scatter_both(sums, order)

    def both(chosen):
        return project(chosen, gate_update, near_first), project(chosen, up_update, far_first)

    if all_rows <= 128:
        gate, up = both(scaled)
    else:
        gate, up = lax.map(both, scaled.reshape(-1, 128, depth))
    gate, up, back = lax.optimization_barrier((gate, up, back))
    stream = back.reshape(residual.shape)
    gate = gate.reshape(all_rows, -1).astype(F32) * scale
    up = up.reshape(all_rows, -1).astype(F32) * scale
    hidden = (jax.nn.silu(gate) * up * coefs[:, None]).astype(BF16)
    out = jnp.dot(hidden, down_weight[0], preferred_element_type=F32).astype(BF16)
    out = out.reshape(pair, ring, own, width).swapaxes(0, 1)
    middle = width // 2
    mixed = jnp.concatenate(
        [scatter_both(out[..., :middle], near_first), scatter_both(out[..., middle:], far_first)],
        axis=1,
    ).reshape(residual.shape)
    return (stream, mixed)


def solution(mesh):
    in_specs = (
        P(None, ("expert", "dp"), None),
        P(None, ("expert", "dp"), None),
        P("expert", "dp", None),
        P("expert", None),
        P(),
        P(None, ("group", "dp"), "expert", None),
        P(None, ("group", "dp"), "expert", None),
        P(None, ("group", "dp"), "expert", None),
        P(None, ("group", "dp"), "expert", None),
        P(("group", "dp"), "expert", None, None),
        P(("group", "dp"), "expert", None, None),
        P(("group", "dp"), "expert"),
        P(None, ("group", "dp"), "expert", None),
        P(None, ("group", "dp"), "expert", None),
    )
    out_specs = (P(None, ("group", "dp"), "expert", None), P(None, ("group", "dp"), "expert", None))
    return jax.shard_map(shards, mesh=mesh, in_specs=in_specs, out_specs=out_specs, check_vma=False)
```

```python
import math

import jax
import jax.numpy as jnp
from jax import lax
from jax.sharding import PartitionSpec as P

QUERY_HEADS = 64
KEY_VALUE_HEADS = 4
HEAD_SIZE = 128
F32 = jnp.float32
BF16 = jnp.bfloat16


def scatter_sum(x, axis_name, order):
    count = x.shape[0]
    bits = count.bit_length() - 1
    if bits == 0:
        return x[0]
    me = lax.axis_index(axis_name)
    x = x.reshape((2,) * bits + x.shape[1:])
    left = list(range(bits - 1, -1, -1))
    for bit in order(bits):
        at = left.index(bit)
        left.pop(at)
        mine = (me >> bit) & 1
        keep = lax.dynamic_index_in_dim(x, mine, at, keepdims=False)
        send = lax.dynamic_index_in_dim(x, 1 - mine, at, keepdims=False)
        got = lax.ppermute(send, axis_name, [(i, i ^ (1 << bit)) for i in range(count)])
        x = (keep.astype(F32) + got.astype(F32)).astype(BF16)
    return x


def add_up(x):
    if lax.axis_size("dp") > 1:
        x = lax.psum(x, "dp")
    count = lax.axis_size("expert")
    for bit in range(count.bit_length() - 1):
        x = x + lax.ppermute(x, "expert", [(i, i ^ (1 << bit)) for i in range(count)])
    return x


def near_first(bits):
    return list(range(bits))


def far_first(bits):
    return [0] + list(range(2, bits)) + [1] if bits > 2 else list(range(bits))


def scatter_both(x, order):
    if x.shape[1] > 1:
        x = scatter_sum(jnp.moveaxis(x, 1, 0), "dp", near_first)
    else:
        x = x[:, 0]
    return scatter_sum(x, "expert", order)


def attend(queries, token_keys, token_values, key_rows, value_rows, lengths):
    steps, rows = queries.shape[0], queries.shape[2]
    slots = key_rows.shape[2]
    per = QUERY_HEADS // KEY_VALUE_HEADS
    q = queries[:, 0].reshape(steps, rows, KEY_VALUE_HEADS, per, HEAD_SIZE)
    kc = key_rows[0].reshape(rows, slots, KEY_VALUE_HEADS, HEAD_SIZE)
    vc = value_rows[0].reshape(rows, slots, KEY_VALUE_HEADS, HEAD_SIZE)
    kt = token_keys[:, 0].reshape(steps, rows, KEY_VALUE_HEADS, HEAD_SIZE)
    vt = token_values[:, 0].reshape(steps, rows, KEY_VALUE_HEADS, HEAD_SIZE)
    scale = 1.0 / math.sqrt(HEAD_SIZE)
    sc = jnp.einsum("srhgd,rlhd->rhsgl", q, kc, preferred_element_type=F32) * scale
    sf = jnp.einsum("srhgd,lrhd->rhsgl", q, kt, preferred_element_type=F32) * scale
    valid = jnp.arange(slots, dtype=jnp.int32)[None, :] < lengths[0][:, None]
    causal = jnp.arange(steps)[None, :] <= jnp.arange(steps)[:, None]
    sc = jnp.where(valid[:, None, None, None, :], sc, -1e30)
    sf = jnp.where(causal[None, None, :, None, :], sf, -1e30)
    peak = jnp.maximum(jnp.max(sc, -1, keepdims=True), jnp.max(sf, -1, keepdims=True))
    ec, ef = jnp.exp(sc - peak), jnp.exp(sf - peak)
    total = jnp.sum(ec, -1, keepdims=True) + jnp.sum(ef, -1, keepdims=True)
    wc, wf = (ec / total).astype(BF16), (ef / total).astype(BF16)
    out = jnp.einsum("rhsgl,rlhd->srhgd", wc, vc, preferred_element_type=F32)
    out = out + jnp.einsum("rhsgl,lrhd->srhgd", wf, vt, preferred_element_type=F32)
    return out.astype(BF16).reshape(steps * rows, QUERY_HEADS * HEAD_SIZE)


def shards(
    gate_update,
    up_update,
    down_weight,
    out_proj,
    norm_gain,
    residual,
    queries,
    token_keys,
    token_values,
    cached_key_rows,
    cached_value_rows,
    lengths,
    expert_ids,
    gate_probs,
):
    experts, depth, units = gate_update.shape
    ring = lax.axis_size("expert")
    pair = lax.axis_size("dp")
    steps, _, rows, width = residual.shape
    top = expert_ids.shape[3]
    own = steps * rows
    me, half = lax.axis_index("expert"), lax.axis_index("dp")

    ids = expert_ids.reshape(own, top)
    probs = gate_probs.reshape(own, top)
    match = ids[:, :, None] == jnp.arange(experts, dtype=jnp.int32)[None, None, :]
    coefs = jnp.sum(jnp.where(match, probs[:, :, None], 0.0), axis=1)
    coarse = coefs.astype(BF16)
    fine = (coefs - coarse.astype(F32)).astype(BF16)
    lanes = -(-2 * experts // 128) * 128
    extra = jnp.pad(jnp.concatenate([coarse, fine], axis=1), ((0, 0), (0, lanes - 2 * experts)))

    attended = attend(queries, token_keys, token_values, cached_key_rows, cached_value_rows, lengths)
    packed = jnp.concatenate(
        [attended.reshape(own, ring, -1), jnp.broadcast_to(extra[:, None], (own, ring, lanes))], axis=2
    )
    spread = lax.all_to_all(
        packed.reshape(own, -1), "expert", split_axis=1, concat_axis=0, tiled=True
    )
    heads = out_proj.shape[0]
    coefs = spread[:, heads:].astype(F32)
    coefs = coefs[:, :experts] + coefs[:, experts : 2 * experts]
    coefs = lax.dynamic_index_in_dim(coefs, me, 1, keepdims=False)
    if pair > 1:
        coefs = lax.all_gather(coefs, "dp", axis=0, tiled=True)
    spread = spread[:, :heads]
    partial = jnp.dot(spread, out_proj, preferred_element_type=F32)
    place = (jnp.arange(ring) == me).astype(F32)
    partial = partial.reshape(ring, own, width) + place[:, None, None] * residual.reshape(1, own, width).astype(F32)
    partial = partial.astype(BF16).reshape(ring * own, ring, width // ring).swapaxes(0, 1)
    middle = partial.shape[1] // 2
    columns = jnp.concatenate(
        [
            scatter_sum(partial[:, :middle], "expert", near_first),
            scatter_sum(partial[:, middle:], "expert", far_first),
        ],
        axis=0,
    )
    back = lax.all_to_all(columns, "expert", split_axis=0, concat_axis=1, tiled=True)
    if pair > 1:
        columns = lax.all_to_all(columns, "dp", split_axis=1, concat_axis=0, tiled=True)

    wide = columns.astype(F32)
    square = add_up(jnp.sum(wide * wide, axis=1))
    gain = lax.dynamic_slice_in_dim(norm_gain, (me * pair + half) * depth, depth)
    scaled = (wide * gain[None, :]).astype(BF16)
    all_rows = scaled.shape[0]

    def project(chosen, weight):
        sums = jnp.einsum("rd,edf->erf", chosen, weight, preferred_element_type=F32).astype(BF16)
        return sums.reshape(experts, chosen.shape[0], pair, units // pair).swapaxes(1, 2)

    def both(chosen, total):
        gate, up = project(chosen, gate_update), project(chosen, up_update)
        gate, up, total = lax.optimization_barrier((gate, up, total))
        return scatter_both(gate, near_first), scatter_both(up, far_first), total

    if all_rows <= 128:
        gate, up, square = both(scaled, square)
    else:
        gate, up = lax.map(lambda chosen: both(chosen, square)[:2], scaled.reshape(-1, 128, depth))
    scale = lax.rsqrt(square / width + 1e-6)[:, None]
    gate, up, back = lax.optimization_barrier((gate, up, back))
    stream = back.reshape(residual.shape)
    gate = gate.reshape(all_rows, -1).astype(F32) * scale
    up = up.reshape(all_rows, -1).astype(F32) * scale
    hidden = (jax.nn.silu(gate) * up * coefs[:, None]).astype(BF16)
    out = jnp.dot(hidden, down_weight[0], preferred_element_type=F32).astype(BF16)
    out = out.reshape(pair, ring, own, width).swapaxes(0, 1)
    middle = width // 2
    mixed = jnp.concatenate(
        [scatter_both(out[..., :middle], near_first), scatter_both(out[..., middle:], far_first)],
        axis=1,
    ).reshape(residual.shape)
    return (stream, mixed)


def solution(mesh):
    in_specs = (
        P(None, ("expert", "dp"), None),
        P(None, ("expert", "dp"), None),
        P("expert", "dp", None),
        P("expert", None),
        P(),
        P(None, ("group", "dp"), "expert", None),
        P(None, ("group", "dp"), "expert", None),
        P(None, ("group", "dp"), "expert", None),
        P(None, ("group", "dp"), "expert", None),
        P(("group", "dp"), "expert", None, None),
        P(("group", "dp"), "expert", None, None),
        P(("group", "dp"), "expert"),
        P(None, ("group", "dp"), "expert", None),
        P(None, ("group", "dp"), "expert", None),
    )
    out_specs = (P(None, ("group", "dp"), "expert", None), P(None, ("group", "dp"), "expert", None))
    return jax.shard_map(shards, mesh=mesh, in_specs=in_specs, out_specs=out_specs, check_vma=False)
```

```python
import math

import jax
import jax.numpy as jnp
from jax import lax
from jax.sharding import PartitionSpec as P

QUERY_HEADS = 64
KEY_VALUE_HEADS = 4
HEAD_SIZE = 128
F32 = jnp.float32
BF16 = jnp.bfloat16


def scatter_sum(x, axis_name, order):
    count = x.shape[0]
    bits = count.bit_length() - 1
    if bits == 0:
        return x[0]
    me = lax.axis_index(axis_name)
    x = x.reshape((2,) * bits + x.shape[1:])
    left = list(range(bits - 1, -1, -1))
    for bit in order(bits):
        at = left.index(bit)
        left.pop(at)
        mine = (me >> bit) & 1
        keep = lax.dynamic_index_in_dim(x, mine, at, keepdims=False)
        send = lax.dynamic_index_in_dim(x, 1 - mine, at, keepdims=False)
        got = lax.ppermute(send, axis_name, [(i, i ^ (1 << bit)) for i in range(count)])
        x = (keep.astype(F32) + got.astype(F32)).astype(BF16)
    return x


def add_up(x):
    if lax.axis_size("dp") > 1:
        x = lax.psum(x, "dp")
    count = lax.axis_size("expert")
    for bit in range(count.bit_length() - 1):
        x = x + lax.ppermute(x, "expert", [(i, i ^ (1 << bit)) for i in range(count)])
    return x


def near_first(bits):
    return list(range(bits))


def far_first(bits):
    return [0] + list(range(2, bits)) + [1] if bits > 2 else list(range(bits))


def scatter_both(x, order):
    if x.shape[1] > 1:
        x = scatter_sum(jnp.moveaxis(x, 1, 0), "dp", near_first)
    else:
        x = x[:, 0]
    return scatter_sum(x, "expert", order)


def attend(queries, token_keys, token_values, key_rows, value_rows, lengths):
    steps, rows = queries.shape[0], queries.shape[2]
    slots = key_rows.shape[2]
    per = QUERY_HEADS // KEY_VALUE_HEADS
    q = queries[:, 0].reshape(steps, rows, KEY_VALUE_HEADS, per, HEAD_SIZE)
    kc = key_rows[0].reshape(rows, slots, KEY_VALUE_HEADS, HEAD_SIZE)
    vc = value_rows[0].reshape(rows, slots, KEY_VALUE_HEADS, HEAD_SIZE)
    kt = token_keys[:, 0].reshape(steps, rows, KEY_VALUE_HEADS, HEAD_SIZE)
    vt = token_values[:, 0].reshape(steps, rows, KEY_VALUE_HEADS, HEAD_SIZE)
    scale = 1.0 / math.sqrt(HEAD_SIZE)
    sc = jnp.einsum("srhgd,rlhd->rhsgl", q, kc, preferred_element_type=F32) * scale
    sf = jnp.einsum("srhgd,lrhd->rhsgl", q, kt, preferred_element_type=F32) * scale
    valid = jnp.arange(slots, dtype=jnp.int32)[None, :] < lengths[0][:, None]
    causal = jnp.arange(steps)[None, :] <= jnp.arange(steps)[:, None]
    sc = jnp.where(valid[:, None, None, None, :], sc, -1e30)
    sf = jnp.where(causal[None, None, :, None, :], sf, -1e30)
    peak = jnp.maximum(jnp.max(sc, -1, keepdims=True), jnp.max(sf, -1, keepdims=True))
    ec, ef = jnp.exp(sc - peak), jnp.exp(sf - peak)
    total = jnp.sum(ec, -1, keepdims=True) + jnp.sum(ef, -1, keepdims=True)
    wc, wf = (ec / total).astype(BF16), (ef / total).astype(BF16)
    out = jnp.einsum("rhsgl,rlhd->srhgd", wc, vc, preferred_element_type=F32)
    out = out + jnp.einsum("rhsgl,lrhd->srhgd", wf, vt, preferred_element_type=F32)
    return out.astype(BF16).reshape(steps * rows, QUERY_HEADS * HEAD_SIZE)


def shards(
    gate_update,
    up_update,
    down_weight,
    out_proj,
    norm_gain,
    residual,
    queries,
    token_keys,
    token_values,
    cached_key_rows,
    cached_value_rows,
    lengths,
    expert_ids,
    gate_probs,
):
    experts, depth, units = gate_update.shape
    ring = lax.axis_size("expert")
    pair = lax.axis_size("dp")
    steps, _, rows, width = residual.shape
    top = expert_ids.shape[3]
    own = steps * rows
    me, half = lax.axis_index("expert"), lax.axis_index("dp")

    ids = expert_ids.reshape(own, top)
    probs = gate_probs.reshape(own, top)
    match = ids[:, :, None] == jnp.arange(experts, dtype=jnp.int32)[None, None, :]
    coefs = jnp.sum(jnp.where(match, probs[:, :, None], 0.0), axis=1)
    coarse = coefs.astype(BF16)
    fine = (coefs - coarse.astype(F32)).astype(BF16)
    lanes = -(-2 * experts // 128) * 128
    extra = jnp.pad(jnp.concatenate([coarse, fine], axis=1), ((0, 0), (0, lanes - 2 * experts)))

    attended = attend(queries, token_keys, token_values, cached_key_rows, cached_value_rows, lengths)
    packed = jnp.concatenate(
        [attended.reshape(own, ring, -1), jnp.broadcast_to(extra[:, None], (own, ring, lanes))], axis=2
    )
    spread = lax.all_to_all(
        packed.reshape(own, -1), "expert", split_axis=1, concat_axis=0, tiled=True
    )
    heads = out_proj.shape[0]
    coefs = spread[:, heads:].astype(F32)
    coefs = coefs[:, :experts] + coefs[:, experts : 2 * experts]
    if pair > 1:
        coefs = lax.all_gather(coefs, "dp", axis=0, tiled=True)
    spread = spread[:, :heads]
    partial = jnp.dot(spread, out_proj, preferred_element_type=F32)
    place = (jnp.arange(ring) == me).astype(F32)
    partial = partial.reshape(ring, own, width) + place[:, None, None] * residual.reshape(1, own, width).astype(F32)
    partial = partial.astype(BF16).reshape(ring * own, ring, width // ring).swapaxes(0, 1)
    middle = partial.shape[1] // 2
    columns = jnp.concatenate(
        [
            scatter_sum(partial[:, :middle], "expert", near_first),
            scatter_sum(partial[:, middle:], "expert", far_first),
        ],
        axis=0,
    )
    back = lax.all_to_all(columns, "expert", split_axis=0, concat_axis=1, tiled=True)
    if pair > 1:
        columns = lax.all_to_all(columns, "dp", split_axis=1, concat_axis=0, tiled=True)

    wide = columns.astype(F32)
    square = add_up(jnp.sum(wide * wide, axis=1))
    gain = lax.dynamic_slice_in_dim(norm_gain, (me * pair + half) * depth, depth)
    scaled = (wide * gain[None, :]).astype(BF16)
    all_rows = scaled.shape[0]

    cap = min(rows, max(2, 3 * rows * top // (2 * experts)))
    present = (coefs > 0).astype(jnp.int32).reshape(-1, rows, experts)
    rank = jnp.cumsum(present, axis=1) - present
    blocks = present.shape[0]
    slot = jnp.where(present > 0, jnp.arange(blocks)[:, None, None] * cap + rank, -1)
    slot = slot.reshape(all_rows, experts).T
    slots = blocks * cap
    select = slot[:, None, :] == jnp.arange(slots)[None, :, None]
    chosen = jnp.einsum("esr,rd->esd", select.astype(BF16), scaled, preferred_element_type=F32)
    chosen = chosen.astype(BF16)

    def project(chosen, weight):
        sums = jnp.einsum("esd,edf->esf", chosen, weight, preferred_element_type=F32).astype(BF16)
        return sums.reshape(experts, chosen.shape[1], pair, units // pair).swapaxes(1, 2)

    def both(chosen, total):
        gate, up = project(chosen, gate_update), project(chosen, up_update)
        gate, up, total = lax.optimization_barrier((gate, up, total))
        cut = chosen.shape[1] // 2
        gate = scatter_both(gate, near_first)
        first = scatter_both(up[:, :, :cut], near_first)
        second = scatter_both(up[:, :, cut:], far_first)
        return gate, jnp.concatenate([first, second], axis=0), total

    if slots <= 128:
        gate, up, square = both(chosen, square)
    else:
        parts = chosen.reshape(experts, -1, 128, depth).swapaxes(0, 1)
        gate, up = lax.map(lambda part: both(part, square)[:2], parts)
    scale = lax.rsqrt(square / width + 1e-6)
    gate, up, back = lax.optimization_barrier((gate, up, back))
    stream = back.reshape(residual.shape)
    mine = lax.dynamic_index_in_dim(select, me, 0, keepdims=False)
    weight = lax.dynamic_index_in_dim(coefs, me, 1, keepdims=False)
    scale = jnp.sum(jnp.where(mine, scale[None, :], 0.0), axis=1, keepdims=True)
    weight = jnp.sum(jnp.where(mine, weight[None, :], 0.0), axis=1, keepdims=True)
    gate = gate.reshape(slots, -1).astype(F32) * scale
    up = up.reshape(slots, -1).astype(F32) * scale
    hidden = (jax.nn.silu(gate) * up * weight).astype(BF16)
    hidden = jnp.einsum("sr,sf->rf", mine.astype(BF16), hidden, preferred_element_type=F32)
    hidden = hidden.astype(BF16)
    out = jnp.dot(hidden, down_weight[0], preferred_element_type=F32).astype(BF16)
    out = out.reshape(pair, ring, own, width).swapaxes(0, 1)
    middle = width // 2
    mixed = jnp.concatenate(
        [scatter_both(out[..., :middle], near_first), scatter_both(out[..., middle:], far_first)],
        axis=1,
    ).reshape(residual.shape)
    return (stream, mixed)


def solution(mesh):
    in_specs = (
        P(None, ("expert", "dp"), None),
        P(None, ("expert", "dp"), None),
        P("expert", "dp", None),
        P("expert", None),
        P(),
        P(None, ("group", "dp"), "expert", None),
        P(None, ("group", "dp"), "expert", None),
        P(None, ("group", "dp"), "expert", None),
        P(None, ("group", "dp"), "expert", None),
        P(("group", "dp"), "expert", None, None),
        P(("group", "dp"), "expert", None, None),
        P(("group", "dp"), "expert"),
        P(None, ("group", "dp"), "expert", None),
        P(None, ("group", "dp"), "expert", None),
    )
    out_specs = (P(None, ("group", "dp"), "expert", None), P(None, ("group", "dp"), "expert", None))
    return jax.shard_map(shards, mesh=mesh, in_specs=in_specs, out_specs=out_specs, check_vma=False)
```

```python
import math

import jax
import jax.numpy as jnp
from jax import lax
from jax.sharding import PartitionSpec as P

QUERY_HEADS = 64
KEY_VALUE_HEADS = 4
HEAD_SIZE = 128
F32 = jnp.float32
BF16 = jnp.bfloat16


def scatter_sum(x, axis_name, order):
    count = x.shape[0]
    bits = count.bit_length() - 1
    if bits == 0:
        return x[0]
    me = lax.axis_index(axis_name)
    x = x.reshape((2,) * bits + x.shape[1:])
    left = list(range(bits - 1, -1, -1))
    for bit in order(bits):
        at = left.index(bit)
        left.pop(at)
        mine = (me >> bit) & 1
        keep = lax.dynamic_index_in_dim(x, mine, at, keepdims=False)
        send = lax.dynamic_index_in_dim(x, 1 - mine, at, keepdims=False)
        got = lax.ppermute(send, axis_name, [(i, i ^ (1 << bit)) for i in range(count)])
        x = (keep.astype(F32) + got.astype(F32)).astype(BF16)
    return x


def add_up(x):
    if lax.axis_size("dp") > 1:
        x = lax.psum(x, "dp")
    count = lax.axis_size("expert")
    for bit in range(count.bit_length() - 1):
        x = x + lax.ppermute(x, "expert", [(i, i ^ (1 << bit)) for i in range(count)])
    return x


def near_first(bits):
    return list(range(bits))


def far_first(bits):
    return [0] + list(range(2, bits)) + [1] if bits > 2 else list(range(bits))


def scatter_both(x, order):
    if x.shape[1] > 1:
        x = scatter_sum(jnp.moveaxis(x, 1, 0), "dp", near_first)
    else:
        x = x[:, 0]
    return scatter_sum(x, "expert", order)


def attend(queries, token_keys, token_values, key_rows, value_rows, lengths):
    steps, rows = queries.shape[0], queries.shape[2]
    slots = key_rows.shape[2]
    per = QUERY_HEADS // KEY_VALUE_HEADS
    q = queries[:, 0].reshape(steps, rows, KEY_VALUE_HEADS, per, HEAD_SIZE)
    kc = key_rows[0].reshape(rows, slots, KEY_VALUE_HEADS, HEAD_SIZE)
    vc = value_rows[0].reshape(rows, slots, KEY_VALUE_HEADS, HEAD_SIZE)
    kt = token_keys[:, 0].reshape(steps, rows, KEY_VALUE_HEADS, HEAD_SIZE)
    vt = token_values[:, 0].reshape(steps, rows, KEY_VALUE_HEADS, HEAD_SIZE)
    scale = 1.0 / math.sqrt(HEAD_SIZE)
    sc = jnp.einsum("srhgd,rlhd->rhsgl", q, kc, preferred_element_type=F32) * scale
    sf = jnp.einsum("srhgd,lrhd->rhsgl", q, kt, preferred_element_type=F32) * scale
    valid = jnp.arange(slots, dtype=jnp.int32)[None, :] < lengths[0][:, None]
    causal = jnp.arange(steps)[None, :] <= jnp.arange(steps)[:, None]
    sc = jnp.where(valid[:, None, None, None, :], sc, -1e30)
    sf = jnp.where(causal[None, None, :, None, :], sf, -1e30)
    peak = jnp.maximum(jnp.max(sc, -1, keepdims=True), jnp.max(sf, -1, keepdims=True))
    ec, ef = jnp.exp(sc - peak), jnp.exp(sf - peak)
    total = jnp.sum(ec, -1, keepdims=True) + jnp.sum(ef, -1, keepdims=True)
    wc, wf = (ec / total).astype(BF16), (ef / total).astype(BF16)
    out = jnp.einsum("rhsgl,rlhd->srhgd", wc, vc, preferred_element_type=F32)
    out = out + jnp.einsum("rhsgl,lrhd->srhgd", wf, vt, preferred_element_type=F32)
    return out.astype(BF16).reshape(steps * rows, QUERY_HEADS * HEAD_SIZE)


def shards(
    gate_update,
    up_update,
    down_weight,
    out_proj,
    norm_gain,
    residual,
    queries,
    token_keys,
    token_values,
    cached_key_rows,
    cached_value_rows,
    lengths,
    expert_ids,
    gate_probs,
):
    experts, depth, units = gate_update.shape
    ring = lax.axis_size("expert")
    pair = lax.axis_size("dp")
    steps, _, rows, width = residual.shape
    top = expert_ids.shape[3]
    own = steps * rows
    me, half = lax.axis_index("expert"), lax.axis_index("dp")

    ids = expert_ids.reshape(own, top)
    probs = gate_probs.reshape(own, top)
    match = ids[:, :, None] == jnp.arange(experts, dtype=jnp.int32)[None, None, :]
    coefs = jnp.sum(jnp.where(match, probs[:, :, None], 0.0), axis=1)
    coarse = coefs.astype(BF16)
    fine = (coefs - coarse.astype(F32)).astype(BF16)
    lanes = -(-2 * experts // 128) * 128
    extra = jnp.pad(jnp.concatenate([coarse, fine], axis=1), ((0, 0), (0, lanes - 2 * experts)))

    attended = attend(queries, token_keys, token_values, cached_key_rows, cached_value_rows, lengths)
    packed = jnp.concatenate(
        [attended.reshape(own, ring, -1), jnp.broadcast_to(extra[:, None], (own, ring, lanes))], axis=2
    )
    spread = lax.all_to_all(
        packed.reshape(own, -1), "expert", split_axis=1, concat_axis=0, tiled=True
    )
    heads = out_proj.shape[0]
    coefs = spread[:, heads:].astype(F32)
    coefs = coefs[:, :experts] + coefs[:, experts : 2 * experts]
    if pair > 1:
        coefs = lax.all_gather(coefs, "dp", axis=0, tiled=True)
    spread = spread[:, :heads]
    partial = jnp.dot(spread, out_proj, preferred_element_type=F32)
    place = (jnp.arange(ring) == me).astype(F32)
    partial = partial.reshape(ring, own, width) + place[:, None, None] * residual.reshape(1, own, width).astype(F32)
    partial = partial.astype(BF16).reshape(ring * own, ring, width // ring).swapaxes(0, 1)
    middle = partial.shape[1] // 2
    columns = jnp.concatenate(
        [
            scatter_sum(partial[:, :middle], "expert", near_first),
            scatter_sum(partial[:, middle:], "expert", far_first),
        ],
        axis=0,
    )
    spans = columns
    if pair > 1:
        spans = lax.all_to_all(columns, "dp", split_axis=1, concat_axis=0, tiled=True)

    wide = spans.astype(F32)
    square = add_up(jnp.sum(wide * wide, axis=1))
    gain = lax.dynamic_slice_in_dim(norm_gain, (me * pair + half) * depth, depth)
    scaled = (wide * gain[None, :]).astype(BF16)
    all_rows = scaled.shape[0]

    cap = min(rows, max(2, 3 * rows * top // (2 * experts)))
    present = (coefs > 0).astype(jnp.int32).reshape(-1, rows, experts)
    rank = jnp.cumsum(present, axis=1) - present
    blocks = present.shape[0]
    slot = jnp.where(present > 0, jnp.arange(blocks)[:, None, None] * cap + rank, -1)
    slot = slot.reshape(all_rows, experts).T
    slots = blocks * cap
    select = slot[:, None, :] == jnp.arange(slots)[None, :, None]
    chosen = jnp.einsum("esr,rd->esd", select.astype(BF16), scaled, preferred_element_type=F32)
    chosen = chosen.astype(BF16)

    def project(chosen, weight):
        sums = jnp.einsum("esd,edf->esf", chosen, weight, preferred_element_type=F32).astype(BF16)
        return sums.reshape(experts, chosen.shape[1], pair, units // pair).swapaxes(1, 2)

    def both(chosen, total):
        cut = chosen.shape[1] // 2
        gate = project(chosen, gate_update)
        gate, chosen = lax.optimization_barrier((gate, chosen))
        up, total = lax.optimization_barrier((project(chosen, up_update), total))
        last = scatter_both(up[:, :, cut:], far_first)
        gate = [scatter_both(part, near_first) for part in (gate[:, :, :cut], gate[:, :, cut:])]
        up = [scatter_both(up[:, :, :cut], near_first), last]
        return jnp.concatenate(gate, axis=0), jnp.concatenate(up, axis=0), total, last

    if slots <= 128:
        gate, up, square, last = both(chosen, square)
        columns, last = lax.optimization_barrier((columns, last))
    else:
        parts = chosen.reshape(experts, -1, 128, depth).swapaxes(0, 1)
        gate, up = lax.map(lambda part: both(part, square)[:2], parts)
    back = lax.all_to_all(columns, "expert", split_axis=0, concat_axis=1, tiled=True)
    scale = lax.rsqrt(square / width + 1e-6)
    gate, up, back = lax.optimization_barrier((gate, up, back))
    stream = back.reshape(residual.shape)
    mine = lax.dynamic_index_in_dim(select, me, 0, keepdims=False)
    weight = lax.dynamic_index_in_dim(coefs, me, 1, keepdims=False)
    scale = jnp.sum(jnp.where(mine, scale[None, :], 0.0), axis=1, keepdims=True)
    weight = jnp.sum(jnp.where(mine, weight[None, :], 0.0), axis=1, keepdims=True)
    gate = gate.reshape(slots, -1).astype(F32) * scale
    up = up.reshape(slots, -1).astype(F32) * scale
    hidden = (jax.nn.silu(gate) * up * weight).astype(BF16)
    hidden = jnp.einsum("sr,sf->rf", mine.astype(BF16), hidden, preferred_element_type=F32)
    hidden = hidden.astype(BF16)
    out = jnp.dot(hidden, down_weight[0], preferred_element_type=F32).astype(BF16)
    out = out.reshape(pair, ring, own, width).swapaxes(0, 1)
    middle = width // 2
    mixed = jnp.concatenate(
        [scatter_both(out[..., :middle], near_first), scatter_both(out[..., middle:], far_first)],
        axis=1,
    ).reshape(residual.shape)
    return (stream, mixed)


def solution(mesh):
    in_specs = (
        P(None, ("expert", "dp"), None),
        P(None, ("expert", "dp"), None),
        P("expert", "dp", None),
        P("expert", None),
        P(),
        P(None, ("group", "dp"), "expert", None),
        P(None, ("group", "dp"), "expert", None),
        P(None, ("group", "dp"), "expert", None),
        P(None, ("group", "dp"), "expert", None),
        P(("group", "dp"), "expert", None, None),
        P(("group", "dp"), "expert", None, None),
        P(("group", "dp"), "expert"),
        P(None, ("group", "dp"), "expert", None),
        P(None, ("group", "dp"), "expert", None),
    )
    out_specs = (P(None, ("group", "dp"), "expert", None), P(None, ("group", "dp"), "expert", None))
    return jax.shard_map(shards, mesh=mesh, in_specs=in_specs, out_specs=out_specs, check_vma=False)
```

```python
import math

import jax
import jax.numpy as jnp
from jax import lax
from jax.sharding import PartitionSpec as P

QUERY_HEADS = 64
KEY_VALUE_HEADS = 4
HEAD_SIZE = 128
F32 = jnp.float32
BF16 = jnp.bfloat16


def scatter_sum(x, axis_name, order, trail=None):
    count = x.shape[0]
    bits = count.bit_length() - 1
    if bits == 0:
        return x[0]
    me = lax.axis_index(axis_name)
    x = x.reshape((2,) * bits + x.shape[1:])
    left = list(range(bits - 1, -1, -1))
    for bit in order(bits):
        at = left.index(bit)
        left.pop(at)
        mine = (me >> bit) & 1
        keep = lax.dynamic_index_in_dim(x, mine, at, keepdims=False)
        send = lax.dynamic_index_in_dim(x, 1 - mine, at, keepdims=False)
        got = lax.ppermute(send, axis_name, [(i, i ^ (1 << bit)) for i in range(count)])
        x = (keep.astype(F32) + got.astype(F32)).astype(BF16)
        if trail is not None:
            trail.append(x)
    return x


def add_up(x):
    if lax.axis_size("dp") > 1:
        x = lax.psum(x, "dp")
    count = lax.axis_size("expert")
    for bit in range(count.bit_length() - 1):
        x = x + lax.ppermute(x, "expert", [(i, i ^ (1 << bit)) for i in range(count)])
    return x


def near_first(bits):
    return list(range(bits))


def far_first(bits):
    return [0] + list(range(2, bits)) + [1] if bits > 2 else list(range(bits))


def scatter_both(x, order, trail=None):
    if x.shape[1] > 1:
        x = scatter_sum(jnp.moveaxis(x, 1, 0), "dp", near_first)
    else:
        x = x[:, 0]
    return scatter_sum(x, "expert", order, trail)


def attend(queries, token_keys, token_values, key_rows, value_rows, lengths):
    steps, rows = queries.shape[0], queries.shape[2]
    slots = key_rows.shape[2]
    per = QUERY_HEADS // KEY_VALUE_HEADS
    q = queries[:, 0].reshape(steps, rows, KEY_VALUE_HEADS, per, HEAD_SIZE)
    kc = key_rows[0].reshape(rows, slots, KEY_VALUE_HEADS, HEAD_SIZE)
    vc = value_rows[0].reshape(rows, slots, KEY_VALUE_HEADS, HEAD_SIZE)
    kt = token_keys[:, 0].reshape(steps, rows, KEY_VALUE_HEADS, HEAD_SIZE)
    vt = token_values[:, 0].reshape(steps, rows, KEY_VALUE_HEADS, HEAD_SIZE)
    scale = 1.0 / math.sqrt(HEAD_SIZE)
    sc = jnp.einsum("srhgd,rlhd->rhsgl", q, kc, preferred_element_type=F32) * scale
    sf = jnp.einsum("srhgd,lrhd->rhsgl", q, kt, preferred_element_type=F32) * scale
    valid = jnp.arange(slots, dtype=jnp.int32)[None, :] < lengths[0][:, None]
    causal = jnp.arange(steps)[None, :] <= jnp.arange(steps)[:, None]
    sc = jnp.where(valid[:, None, None, None, :], sc, -1e30)
    sf = jnp.where(causal[None, None, :, None, :], sf, -1e30)
    peak = jnp.maximum(jnp.max(sc, -1, keepdims=True), jnp.max(sf, -1, keepdims=True))
    ec, ef = jnp.exp(sc - peak), jnp.exp(sf - peak)
    total = jnp.sum(ec, -1, keepdims=True) + jnp.sum(ef, -1, keepdims=True)
    wc, wf = (ec / total).astype(BF16), (ef / total).astype(BF16)
    out = jnp.einsum("rhsgl,rlhd->srhgd", wc, vc, preferred_element_type=F32)
    out = out + jnp.einsum("rhsgl,lrhd->srhgd", wf, vt, preferred_element_type=F32)
    return out.astype(BF16).reshape(steps * rows, QUERY_HEADS * HEAD_SIZE)


def shards(
    gate_update,
    up_update,
    down_weight,
    out_proj,
    norm_gain,
    residual,
    queries,
    token_keys,
    token_values,
    cached_key_rows,
    cached_value_rows,
    lengths,
    expert_ids,
    gate_probs,
):
    experts, depth, units = gate_update.shape
    ring = lax.axis_size("expert")
    pair = lax.axis_size("dp")
    steps, _, rows, width = residual.shape
    top = expert_ids.shape[3]
    own = steps * rows
    me, half = lax.axis_index("expert"), lax.axis_index("dp")

    ids = expert_ids.reshape(own, top)
    probs = gate_probs.reshape(own, top)
    match = ids[:, :, None] == jnp.arange(experts, dtype=jnp.int32)[None, None, :]
    coefs = jnp.sum(jnp.where(match, probs[:, :, None], 0.0), axis=1)
    coarse = coefs.astype(BF16)
    fine = (coefs - coarse.astype(F32)).astype(BF16)
    lanes = -(-2 * experts // 128) * 128
    extra = jnp.pad(jnp.concatenate([coarse, fine], axis=1), ((0, 0), (0, lanes - 2 * experts)))

    attended = attend(queries, token_keys, token_values, cached_key_rows, cached_value_rows, lengths)
    packed = jnp.concatenate(
        [attended.reshape(own, ring, -1), jnp.broadcast_to(extra[:, None], (own, ring, lanes))], axis=2
    )
    spread = lax.all_to_all(
        packed.reshape(own, -1), "expert", split_axis=1, concat_axis=0, tiled=True
    )
    heads = out_proj.shape[0]
    coefs = spread[:, heads:].astype(F32)
    coefs = coefs[:, :experts] + coefs[:, experts : 2 * experts]
    if pair > 1:
        coefs = lax.all_gather(coefs, "dp", axis=0, tiled=True)
    spread = spread[:, :heads]
    partial = jnp.dot(spread, out_proj, preferred_element_type=F32)
    place = (jnp.arange(ring) == me).astype(F32)
    partial = partial.reshape(ring, own, width) + place[:, None, None] * residual.reshape(1, own, width).astype(F32)
    partial = partial.astype(BF16).reshape(ring * own, ring, width // ring).swapaxes(0, 1)
    middle = partial.shape[1] // 2
    columns = jnp.concatenate(
        [
            scatter_sum(partial[:, :middle], "expert", near_first),
            scatter_sum(partial[:, middle:], "expert", far_first),
        ],
        axis=0,
    )
    spans = columns
    if pair > 1:
        spans = lax.all_to_all(columns, "dp", split_axis=1, concat_axis=0, tiled=True)

    wide = spans.astype(F32)
    square = add_up(jnp.sum(wide * wide, axis=1))
    gain = lax.dynamic_slice_in_dim(norm_gain, (me * pair + half) * depth, depth)
    scaled = (wide * gain[None, :]).astype(BF16)
    all_rows = scaled.shape[0]

    cap = min(rows, max(2, 3 * rows * top // (2 * experts)))
    present = (coefs > 0).astype(jnp.int32).reshape(-1, rows, experts)
    rank = jnp.cumsum(present, axis=1) - present
    blocks = present.shape[0]
    slot = jnp.where(present > 0, jnp.arange(blocks)[:, None, None] * cap + rank, -1)
    slot = slot.reshape(all_rows, experts).T
    slots = blocks * cap
    select = slot[:, None, :] == jnp.arange(slots)[None, :, None]
    chosen = jnp.einsum("esr,rd->esd", select.astype(BF16), scaled, preferred_element_type=F32)
    chosen = chosen.astype(BF16)

    def project(chosen, weight):
        sums = jnp.einsum("esd,edf->esf", chosen, weight, preferred_element_type=F32).astype(BF16)
        return sums.reshape(experts, chosen.shape[1], pair, units // pair).swapaxes(1, 2)

    def both(chosen, total):
        cut = chosen.shape[1] // 2
        gate = project(chosen, gate_update)
        gate, chosen = lax.optimization_barrier((gate, chosen))
        up, total = lax.optimization_barrier((project(chosen, up_update), total))
        last = scatter_both(up[:, :, cut:], far_first)
        trail = []
        gate = [
            scatter_both(gate[:, :, :cut], near_first, trail),
            scatter_both(gate[:, :, cut:], near_first),
        ]
        up = [scatter_both(up[:, :, :cut], near_first), last]
        return jnp.concatenate(gate, axis=0), jnp.concatenate(up, axis=0), total, trail[0]

    if slots <= 128:
        gate, up, square, early = both(chosen, square)
        columns, early = lax.optimization_barrier((columns, early))
    else:
        parts = chosen.reshape(experts, -1, 128, depth).swapaxes(0, 1)
        gate, up = lax.map(lambda part: both(part, square)[:2], parts)
    back = lax.all_to_all(columns, "expert", split_axis=0, concat_axis=1, tiled=True)
    scale = lax.rsqrt(square / width + 1e-6)
    gate, up, back = lax.optimization_barrier((gate, up, back))
    stream = back.reshape(residual.shape)
    mine = lax.dynamic_index_in_dim(select, me, 0, keepdims=False)
    weight = lax.dynamic_index_in_dim(coefs, me, 1, keepdims=False)
    scale = jnp.sum(jnp.where(mine, scale[None, :], 0.0), axis=1, keepdims=True)
    weight = jnp.sum(jnp.where(mine, weight[None, :], 0.0), axis=1, keepdims=True)
    gate = gate.reshape(slots, -1).astype(F32) * scale
    up = up.reshape(slots, -1).astype(F32) * scale
    hidden = (jax.nn.silu(gate) * up * weight).astype(BF16)
    hidden = jnp.einsum("sr,sf->rf", mine.astype(BF16), hidden, preferred_element_type=F32)
    hidden = hidden.astype(BF16)
    out = jnp.dot(hidden, down_weight[0], preferred_element_type=F32).astype(BF16)
    out = out.reshape(pair, ring, own, width).swapaxes(0, 1)
    middle = width // 2
    mixed = jnp.concatenate(
        [scatter_both(out[..., :middle], near_first), scatter_both(out[..., middle:], far_first)],
        axis=1,
    ).reshape(residual.shape)
    return (stream, mixed)


def solution(mesh):
    in_specs = (
        P(None, ("expert", "dp"), None),
        P(None, ("expert", "dp"), None),
        P("expert", "dp", None),
        P("expert", None),
        P(),
        P(None, ("group", "dp"), "expert", None),
        P(None, ("group", "dp"), "expert", None),
        P(None, ("group", "dp"), "expert", None),
        P(None, ("group", "dp"), "expert", None),
        P(("group", "dp"), "expert", None, None),
        P(("group", "dp"), "expert", None, None),
        P(("group", "dp"), "expert"),
        P(None, ("group", "dp"), "expert", None),
        P(None, ("group", "dp"), "expert", None),
    )
    out_specs = (P(None, ("group", "dp"), "expert", None), P(None, ("group", "dp"), "expert", None))
    return jax.shard_map(shards, mesh=mesh, in_specs=in_specs, out_specs=out_specs, check_vma=False)
```
